256 devices in a mesh: seq: 32 (over x, y, core), chan: 8 (over z).
Axes of the slice: x: 4, y: 4, z: 8, core: 2. Of those that a mesh axis runs over, the one named last changes fastest.
Arguments:
- query_proj: bfloat16 [16384, 2048], P('seq', 'chan'), may hold values from -6 to 6
- key_proj: bfloat16 [16384, 2048], P('seq', 'chan'), may hold values from -6 to 6
- value_proj: bfloat16 [16384, 2048], P('seq', 'chan'), may hold values from -6 to 6
- short_taps: float32 [3, 3, 2048], P(None, None, 'chan'), may hold values from -1 to 1
- kernel: float32 [16384, 2048], P('seq', 'chan'), may hold values from -1 to 1
- skip: float32 [2048], P('chan'), may hold values from -1 to 1
- out_weight: bfloat16 [2048, 4096], P(None, 'chan'), may hold values from -0.125 to 0.125
Outputs:
- output: bfloat16 [16384, 4096], P('seq', 'chan')
The draws below stay inside these ranges and needn't reach their ends.
All inputs are finite; a program needn't handle non-finite values.
Results may differ from the reference program's by a relative error of at most 0.005.
Values may be sent and summed in bfloat16 or wider, within the bound.
A program may use at most 64 MiB of HBM per device.

```python
import math
import jax
import jax.numpy as jnp

C = 2048
DM = 4096
TOKENS = 16384


def draw_kernel(key, part):
    rate_key = jax.random.fold_in(key, 11)
    noise_key = jax.random.fold_in(key, 12)
    level_key = jax.random.fold_in(key, 13)
    floor_key = jax.random.fold_in(key, 14)
    uniform_part = jax.random.uniform(rate_key, (C,), jnp.float32)
    lower = 0.5 / TOKENS
    upper = 1.0 / 32
    low_log = math.log(lower)
    high_log = math.log(upper)
    rates = jnp.exp(low_log + uniform_part * (high_log - low_log))
    times = jnp.arange(TOKENS).astype(jnp.float32)
    envelope = jnp.sqrt(2.0 * rates)[None, :] * jnp.exp(-rates[None, :] * times[:, None])
    noise = jnp.clip(jax.random.normal(noise_key, (TOKENS, C), jnp.float32), -3.5, 3.5)
    levels = 0.4 + 0.6 * jax.random.uniform(level_key, (C,), jnp.float32)
    spread_level = levels[None, :] * jnp.float32(1.0 / math.sqrt(TOKENS))
    floor_noise = jnp.clip(jax.random.normal(floor_key, (TOKENS, C), jnp.float32), -3.5, 3.5)
    values = envelope * noise + spread_level * floor_noise
    return jnp.clip(values, -1.0, 1.0).astype(jnp.float32)


def block_levels(own_key, shape, split, low, top_value):
    gain, own = 1.0, jax.random.fold_in(own_key, 6)
    for position, parts in split:
        steps = jnp.exp(jax.random.uniform(jax.random.fold_in(own, position), (parts,), jnp.float32, low / len(split), top_value / len(split)))
        gain = gain * jnp.repeat(steps, shape[position] // parts).reshape([-1 if axis == position else 1 for axis in range(len(shape))])
    return gain


def gaussian(stream_key, dims, deviation, limit, cuts=(), kind=jnp.bfloat16):
    entries = deviation * jax.random.normal(stream_key, dims, jnp.float32)
    if cuts:
        entries = entries * block_levels(stream_key, dims, cuts, -0.22, 0.18)
    return jnp.clip(entries, -limit, limit).astype(kind)


def setup_inputs(seed: int = 0) -> dict:
    key_list = jax.random.split(jax.random.key(seed), 8)
    return {
        "query_proj": gaussian(key_list[0], (TOKENS, C), 1.0, 6.0, ((0, 32), (1, 8))),
        "key_proj": gaussian(key_list[1], (TOKENS, C), 1.0, 6.0, ((0, 32), (1, 8))),
        "value_proj": gaussian(key_list[2], (TOKENS, C), 1.0, 6.0, ((0, 32), (1, 8))),
        "short_taps": jnp.clip(jax.random.uniform(key_list[3], (3, 3, C), jnp.float32, -1.0, 1.0) * block_levels(key_list[3], (3, 3, C), ((2, 8),), -0.4, 0.0), -1.0, 1.0),
        "kernel": draw_kernel(jax.random.fold_in(key_list[7], 71), 0),
        "skip": jnp.clip(jax.random.uniform(key_list[5], (C,), jnp.float32, -1.0, 1.0) * block_levels(key_list[5], (C,), ((0, 8),), -0.4, 0.0), -1.0, 1.0),
        "out_weight": gaussian(key_list[6], (C, DM), C ** -0.5, 0.125, ((1, 8),)),
    }


def short_filter(stream, taps):
    extended = jnp.concatenate([jnp.zeros((2, stream.shape[1]), stream.dtype), stream], 0).astype(jnp.float32)
    return taps[0] * extended[2:] + taps[1] * extended[1:-1] + taps[2] * extended[:-2]


def reference(query_proj, key_proj, value_proj, short_taps, kernel, skip, out_weight):
    query_short = short_filter(query_proj, short_taps[:, 0])
    key_short = short_filter(key_proj, short_taps[:, 1])
    value_short = short_filter(value_proj, short_taps[:, 2])
    mixed = key_short * value_short
    length = 2 * TOKENS
    spectrum = jnp.fft.rfft(mixed, n=length, axis=0) * jnp.fft.rfft(kernel, n=length, axis=0)
    conv = jnp.fft.irfft(spectrum, n=length, axis=0)[:TOKENS]
    gated = (query_short * (conv + skip[None, :] * mixed)).astype(jnp.bfloat16)
    return jnp.dot(gated, out_weight, preferred_element_type=jnp.float32).astype(jnp.bfloat16)
```

```python
import functools
import math

import jax
import jax.numpy as jnp
import ml_dtypes
import numpy as np
from jax import lax
from jax.experimental import pallas as pl
from jax.experimental.pallas import tpu as pltpu
from jax.sharding import PartitionSpec as P

LANES = 128
F32 = jnp.float32
BF16 = jnp.bfloat16


def high_low(table):
    high = table.astype(ml_dtypes.bfloat16)
    low = (table - high.astype(np.float64)).astype(ml_dtypes.bfloat16)
    return high, low


def build_tables(outer):
    length = outer * LANES
    position = np.arange(outer)
    lane = np.arange(LANES)
    angle = 2.0 * math.pi / (4 * outer) * ((4 * position[:, None] + 1) * position[None, :] % (4 * outer))
    first = np.concatenate([np.cos(angle), -np.sin(angle)], 0)
    last = np.concatenate([np.cos(angle).T, -np.sin(angle).T], 1) / length
    twist = 2.0 * math.pi / (4 * length) * ((4 * position[:, None] + 1) * lane[None, :] % (4 * length))
    inner = 2.0 * math.pi / LANES * (lane[:, None] * lane[None, :] % LANES)
    cos, sin = np.cos(inner), np.sin(inner)
    forward = np.block([[cos, -sin], [sin, cos]])
    backward = np.block([[cos, sin], [-sin, cos]])
    return (
        np.concatenate(high_low(first), 1),
        np.stack([np.cos(twist), np.sin(twist)]).astype(np.float32),
        np.stack(high_low(forward)),
        np.stack(high_low(backward)),
        np.stack(high_low(last)),
    )


def split(values):
    high = values.astype(BF16)
    return high, (values - high.astype(F32)).astype(BF16)


def dot(lhs, rhs):
    return jnp.dot(lhs, rhs, preferred_element_type=F32)


def operator(
    seq, chan,
    query_hbm, key_hbm, value_hbm, taps_ref, filter_hbm, skip_ref, weight_hbm,
    first_hbm, twist_hbm, forward_hbm, backward_hbm, last_hbm,
    out_ref,
    streams, halo, filt, weight, first, twist, forward, backward, last,
    extended, mixed, gate, stage, send_filter, send_signal, send_conv,
    recv_filter, recv_signal, recv_conv, spectrum, high_ref, low_ref, gathered, total,
    load_sem, halo_sem, send_sem, recv_sem, ring_send, ring_recv,
):
    me = lax.axis_index("seq")
    layer = lax.axis_index("chan")
    tokens = streams.shape[1]
    sub = tokens // LANES
    outer = seq * sub
    groups = streams.shape[2] // LANES
    per = LANES // seq
    block = sub * per
    rows = seq * block

    loads = [
        pltpu.make_async_copy(source, target, load_sem.at[slot])
        for slot, (source, target) in enumerate((
            (filter_hbm, filt),
            (key_hbm, streams.at[1]),
            (value_hbm, streams.at[2]),
            (query_hbm, streams.at[0]),
            (first_hbm, first),
            (twist_hbm, twist),
            (forward_hbm, forward),
            (backward_hbm, backward),
            (last_hbm, last),
            (weight_hbm, weight),
        ))
    ]
    for load in loads:
        load.start()

    barrier = pltpu.get_barrier_semaphore()

    @pl.loop(1, seq)
    def _(step):
        pl.semaphore_signal(barrier, inc=1, device_id={"seq": lax.rem(me + step, seq)})

    right = lax.rem(layer + 1, chan)
    left = lax.rem(layer + chan - 1, chan)
    pl.semaphore_signal(barrier, inc=1, device_id={"chan": right})
    pl.semaphore_signal(barrier, inc=1, device_id={"chan": left})

    def lanes(group):
        return slice(group * LANES, (group + 1) * LANES)

    def scatter(tile, part):
        for channel in range(per):
            stage[pl.ds(part * per + channel, seq, stride=block), :] = tile[channel * seq:(channel + 1) * seq, :]

    def block_of(ref, group, device):
        return ref.at[group, pl.ds(pl.multiple_of(device * block, block), block), :]

    def send_all(source, target, group, slot):
        @pl.loop(1, seq)
        def _(step):
            other = lax.rem(me + step, seq)
            pltpu.make_async_remote_copy(
                src_ref=block_of(source, group, other),
                dst_ref=block_of(target, group, me),
                send_sem=send_sem.at[slot],
                recv_sem=recv_sem.at[slot],
                device_id={"seq": other},
            ).start()

        own = pl.ds(pl.multiple_of(me * block, block), block)
        target[group, own, :] = source[group, own, :]

    def wait_all(ref, group, sem):
        part = ref.at[group, pl.ds(0, (seq - 1) * block), :]
        pltpu.make_async_copy(part, part, sem).wait()

    loads[0].wait()
    for group in range(groups):
        for part in range(sub):
            scatter(filt[part * LANES:(part + 1) * LANES, lanes(group)].T, part)
        send_filter[group] = stage[...].astype(BF16)

    for load in loads[1:4]:
        load.wait()
    pl.semaphore_wait(barrier, seq + 1)
    edge = pltpu.make_async_remote_copy(
        src_ref=streams.at[:, pl.ds(tokens - 16, 16), :],
        dst_ref=halo,
        send_sem=halo_sem.at[0],
        recv_sem=halo_sem.at[1],
        device_id={"seq": lax.rem(me + 1, seq)},
    )
    edge.start()
    for group in range(groups):
        send_all(send_filter, recv_filter, group, group)

    for slot in range(3):
        extended[slot, 16:, :] = streams[slot].astype(F32)
    edge.wait()
    keep = jnp.where(me > 0, 1.0, 0.0).astype(F32)
    for slot in range(3):
        extended[slot, :16, :] = halo[slot].astype(F32) * keep

    def short(slot, part, group):
        base = 16 + part * LANES
        at = lanes(group)
        return (
            taps_ref[0, slot:slot + 1, at] * extended[slot, base:base + LANES, at]
            + taps_ref[1, slot:slot + 1, at] * extended[slot, base - 1:base - 1 + LANES, at]
            + taps_ref[2, slot:slot + 1, at] * extended[slot, base - 2:base - 2 + LANES, at]
        )

    for group in range(groups):
        for part in range(sub):
            tile = short(1, part, group) * short(2, part, group)
            mixed[part * LANES:(part + 1) * LANES, lanes(group)] = tile
            scatter(tile.T, part)
        send_signal[group] = stage[...].astype(BF16)
        send_all(send_signal, recv_signal, group, groups + group)

    for group in range(groups):
        for part in range(sub):
            gate[part * LANES:(part + 1) * LANES, lanes(group)] = short(0, part, group)

    for load in loads[4:9]:
        load.wait()

    def transform(ref, group):
        stage[...] = ref[group].astype(F32)
        for pair in range(per // 2):
            values = jnp.concatenate(
                [stage[pl.ds(2 * pair + side, outer, stride=per), :] for side in range(2)], 1
            ).astype(BF16)
            outer_spec = dot(first[...], jnp.concatenate([values, values], 0))
            for side in range(2):
                real, imag = outer_spec[:outer, lanes(side)], outer_spec[outer:, lanes(side)]
                at = slice((2 * pair + side) * outer, (2 * pair + side + 1) * outer)
                high_ref[at, :LANES], low_ref[at, :LANES] = split(real * twist[0] + imag * twist[1])
                high_ref[at, LANES:], low_ref[at, LANES:] = split(imag * twist[0] - real * twist[1])
        return apply(forward)

    def apply(table):
        high, low = high_ref[...], low_ref[...]
        return dot(high, table[0]) + dot(low, table[0]) + dot(high, table[1])

    for group in range(groups):
        wait_all(recv_filter, group, recv_sem.at[group])
        spectrum[group] = transform(recv_filter, group)

    for group in range(groups):
        wait_all(recv_signal, group, recv_sem.at[groups + group])
        signal = transform(recv_signal, group)
        sig_real, sig_imag = signal[:, :LANES], signal[:, LANES:]
        fil_real, fil_imag = spectrum[group, :, :LANES], spectrum[group, :, LANES:]
        high_ref[:, :LANES], low_ref[:, :LANES] = split(sig_real * fil_real - sig_imag * fil_imag)
        high_ref[:, LANES:], low_ref[:, LANES:] = split(sig_real * fil_imag + sig_imag * fil_real)
        back = apply(backward)
        for pair in range(per // 2):
            sides = []
            for side in range(2):
                at = slice((2 * pair + side) * outer, (2 * pair + side + 1) * outer)
                real, imag = back[at, :LANES], back[at, LANES:]
                sides.append(jnp.concatenate(
                    [real * twist[0] - imag * twist[1], imag * twist[0] + real * twist[1]], 0
                ))
            high, low = split(jnp.concatenate(sides, 1))
            conv = dot(last[0], high) + dot(last[0], low) + dot(last[1], high)
            for side in range(2):
                stage[pl.ds(2 * pair + side, outer, stride=per), :] = conv[:, lanes(side)]
        send_conv[group] = stage[...].astype(BF16)
        send_all(send_conv, recv_conv, group, 2 * groups + group)

    half = tokens // 2
    hops = ((chan // 2, chan - 1 - chan // 2), (chan - 1 - chan // 2, chan // 2))

    def hop(direction, step, group, side):
        origin = lax.rem(layer + (chan - step if direction == 0 else step), chan)
        piece = gathered.at[origin, group, pl.ds(side * half, half), :]
        return pltpu.make_async_remote_copy(
            src_ref=piece,
            dst_ref=piece,
            send_sem=ring_send.at[direction, step, group, side],
            recv_sem=ring_recv.at[direction, step, group, side],
            device_id={"chan": right if direction == 0 else left},
        )

    for group in range(groups):
        wait_all(recv_conv, group, recv_sem.at[2 * groups + group])
        stage[...] = recv_conv[group].astype(F32)
        for part in range(sub):
            conv = jnp.concatenate(
                [stage[pl.ds(part * per + channel, seq, stride=block), :] for channel in range(per)], 0
            ).T
            at = slice(part * LANES, (part + 1) * LANES)
            signal = mixed[at, lanes(group)]
            gated = gate[at, lanes(group)] * (conv + skip_ref[:, lanes(group)] * signal)
            gathered[layer, group, at, :] = gated.astype(BF16)
        for side in range(2):
            for direction in range(2):
                if hops[side][direction] > 0:
                    hop(direction, 0, group, side).start()

    loads[9].wait()

    def project(origin, side, begin):
        at = slice(side * half, (side + 1) * half)
        values = jnp.concatenate([gathered[origin, group, at, :] for group in range(groups)], 1)
        depth = groups * LANES
        product = dot(values, weight[pl.ds(pl.multiple_of(origin * depth, depth), depth), :])
        if begin:
            total[at, :] = product
        else:
            total[at, :] += product

    for side in range(2):
        project(layer, side, True)
    for step in range(1, chan // 2 + 1):
        for group in range(groups):
            for side in range(2):
                for direction in range(2):
                    if step <= hops[side][direction]:
                        hop(direction, step - 1, group, side).wait_recv()
                    if step < hops[side][direction]:
                        hop(direction, step, group, side).start()
        for side in range(2):
            for direction in range(2):
                if step <= hops[side][direction]:
                    origin = lax.rem(layer + (chan - step if direction == 0 else step), chan)
                    project(origin, side, False)
    out_ref[...] = total[...].astype(BF16)

    for group in range(groups):
        for slot, ref in enumerate((send_filter, send_signal, send_conv)):
            wait_all(ref, group, send_sem.at[slot * groups + group])
    for group in range(groups):
        for side in range(2):
            for direction in range(2):
                for step in range(hops[side][direction]):
                    hop(direction, step, group, side).wait_send()


def shards(query_proj, key_proj, value_proj, short_taps, kernel, skip, out_weight):
    seq, chan = lax.axis_size("seq"), lax.axis_size("chan")
    tokens, width = query_proj.shape
    groups = width // LANES
    per = LANES // seq
    outer = seq * tokens // LANES
    rows = outer * per
    features = out_weight.shape[1]
    tables = build_tables(outer)
    anywhere = pl.BlockSpec(memory_space=pl.ANY)
    inside = pl.BlockSpec(memory_space=pltpu.VMEM)
    exchange = pltpu.VMEM((groups, rows, LANES), BF16)
    return pl.pallas_call(
        functools.partial(operator, seq, chan),
        out_shape=jax.ShapeDtypeStruct((tokens, features), BF16),
        in_specs=[anywhere, anywhere, anywhere, inside, anywhere, inside, anywhere] + [anywhere] * 5,
        out_specs=inside,
        scratch_shapes=[
            pltpu.VMEM((3, tokens, width), BF16),
            pltpu.VMEM((3, 16, width), BF16),
            pltpu.VMEM((tokens, width), F32),
            pltpu.VMEM(out_weight.shape, BF16),
            *(pltpu.VMEM(table.shape, table.dtype) for table in tables),
            pltpu.VMEM((3, tokens + 16, width), F32),
            pltpu.VMEM((tokens, width), F32),
            pltpu.VMEM((tokens, width), F32),
            pltpu.VMEM((rows, LANES), F32),
            exchange, exchange, exchange, exchange, exchange, exchange,
            pltpu.VMEM((groups, rows, 2 * LANES), F32),
            pltpu.VMEM((rows, 2 * LANES), BF16),
            pltpu.VMEM((rows, 2 * LANES), BF16),
            pltpu.VMEM((chan, groups, tokens, LANES), BF16),
            pltpu.VMEM((tokens, features), F32),
            pltpu.SemaphoreType.DMA((10,)),
            pltpu.SemaphoreType.DMA((2,)),
            pltpu.SemaphoreType.DMA((3 * groups,)),
            pltpu.SemaphoreType.DMA((3 * groups,)),
            pltpu.SemaphoreType.DMA((2, max(1, chan // 2), groups, 2)),
            pltpu.SemaphoreType.DMA((2, max(1, chan // 2), groups, 2)),
        ],
        compiler_params=pltpu.CompilerParams(
            collective_id=0, has_side_effects=True, vmem_limit_bytes=56 * 1024 * 1024
        ),
        cost_estimate=pl.CostEstimate(flops=2_000_000_000, bytes_accessed=5_000_000, transcendentals=0),
    )(
        query_proj, key_proj, value_proj, short_taps, kernel, skip.reshape(1, width), out_weight,
        *(jnp.asarray(table) for table in tables),
    )


def solution(mesh):
    return jax.shard_map(
        shards,
        mesh=mesh,
        in_specs=(
            P("seq", "chan"),
            P("seq", "chan"),
            P("seq", "chan"),
            P(None, None, "chan"),
            P("seq", "chan"),
            P("chan"),
            P(None, "chan"),
        ),
        out_specs=P("seq", "chan"),
        check_vma=False,
    )
```

```python
import functools
import math

import jax
import jax.numpy as jnp
import ml_dtypes
import numpy as np
from jax import lax
from jax.experimental import pallas as pl
from jax.experimental.pallas import tpu as pltpu
from jax.sharding import PartitionSpec as P

LANES = 128
F32 = jnp.float32
BF16 = jnp.bfloat16
GRIDS = {32: (4, 4, 2), 8: (2, 2, 2), 4: (1, 2, 2)}


def high_low(table):
    high = table.astype(ml_dtypes.bfloat16)
    low = (table - high.astype(np.float64)).astype(ml_dtypes.bfloat16)
    return high, low


def build_tables(outer):
    length = outer * LANES
    position = np.arange(outer)
    lane = np.arange(LANES)
    angle = 2.0 * math.pi / (4 * outer) * ((4 * position[:, None] + 1) * position[None, :] % (4 * outer))
    first = np.concatenate([np.cos(angle), -np.sin(angle)], 0)
    last = np.concatenate([np.cos(angle).T, -np.sin(angle).T], 1) / length
    twist = 2.0 * math.pi / (4 * length) * ((4 * position[:, None] + 1) * lane[None, :] % (4 * length))
    inner = 2.0 * math.pi / LANES * (lane[:, None] * lane[None, :] % LANES)
    cos, sin = np.cos(inner), np.sin(inner)
    forward = np.block([[cos, -sin], [sin, cos]])
    backward = np.block([[cos, sin], [-sin, cos]])
    return (
        np.concatenate(high_low(first), 1),
        np.stack([np.cos(twist), np.sin(twist)]).astype(np.float32),
        np.stack(high_low(forward)),
        np.stack(high_low(backward)),
        np.stack(high_low(last)),
    )


def split(values):
    high = values.astype(BF16)
    return high, (values - high.astype(F32)).astype(BF16)


def dot(lhs, rhs):
    return jnp.dot(lhs, rhs, preferred_element_type=F32)


def peers(me, grid):
    along_x, along_y, cores = grid
    x, y, core = me // (along_y * cores), me // cores % along_y, me % cores
    steps = [(i, j, k) for i in range(along_x) for j in range(along_y) for k in range(cores)][1:]
    steps.sort(key=lambda step: -4 * (min(step[0], along_x - step[0]) + min(step[1], along_y - step[1])) - step[2])
    return [
        ((x + i) % along_x * along_y + (y + j) % along_y) * cores + (core + k) % cores
        for i, j, k in steps
    ]


def operator(
    grid, seq, chan,
    query_hbm, key_hbm, value_hbm, taps_hbm, filter_hbm, skip_hbm, weight_hbm,
    first_hbm, twist_hbm, forward_hbm, backward_hbm, last_hbm,
    out_ref,
    streams, halo, filt, taps_ref, skip_ref, weight, first, twist, forward, backward, last,
    extended, mixed, gate, stage, send_filter, send_signal, send_conv,
    recv_filter, recv_signal, recv_conv, spectrum, high_ref, low_ref, gathered, total,
    load_sem, halo_sem, send_sem, recv_sem, ring_send, ring_recv,
):
    me = lax.axis_index("seq")
    layer = lax.axis_index("chan")
    tokens = streams.shape[1]
    sub = tokens // LANES
    outer = seq * sub
    groups = streams.shape[2] // LANES
    per = LANES // seq
    block = sub * per
    rows = seq * block

    loads = [
        pltpu.make_async_copy(source, target, load_sem.at[slot])
        for slot, (source, target) in enumerate((
            (filter_hbm, filt),
            (key_hbm, streams.at[1]),
            (value_hbm, streams.at[2]),
            (query_hbm, streams.at[0]),
            (taps_hbm, taps_ref),
            (skip_hbm, skip_ref),
            (first_hbm, first),
            (twist_hbm, twist),
            (forward_hbm, forward),
            (backward_hbm, backward),
            (last_hbm, last),
            (weight_hbm, weight),
        ))
    ]
    barrier = pltpu.get_barrier_semaphore()

    others = peers(me, grid)
    for other in others:
        pl.semaphore_signal(barrier, inc=1, device_id={"seq": other})
    right = lax.rem(layer + 1, chan)
    left = lax.rem(layer + chan - 1, chan)
    pl.semaphore_signal(barrier, inc=1, device_id={"chan": right})
    pl.semaphore_signal(barrier, inc=1, device_id={"chan": left})
    for load in loads:
        load.start()

    def lanes(group):
        return slice(group * LANES, (group + 1) * LANES)

    def scatter(tile, part):
        for channel in range(per):
            stage[pl.ds(part * per + channel, seq, stride=block), :] = tile[channel * seq:(channel + 1) * seq, :]

    def block_of(ref, group, device):
        return ref.at[group, pl.ds(pl.multiple_of(device * block, block), block), :]

    def send_all(source, target, group, slot):
        for other in others:
            pltpu.make_async_remote_copy(
                src_ref=block_of(source, group, other),
                dst_ref=block_of(target, group, me),
                send_sem=send_sem.at[slot],
                recv_sem=recv_sem.at[slot],
                device_id={"seq": other},
            ).start()

        own = pl.ds(pl.multiple_of(me * block, block), block)
        target[group, own, :] = source[group, own, :]

    def wait_all(ref, group, sem):
        part = ref.at[group, pl.ds(0, (seq - 1) * block), :]
        pltpu.make_async_copy(part, part, sem).wait()

    loads[0].wait()
    for group in range(groups):
        for part in range(sub):
            scatter(filt[part * LANES:(part + 1) * LANES, lanes(group)].T, part)
        send_filter[group] = stage[...].astype(BF16)

    for load in loads[1:6]:
        load.wait()
    pl.semaphore_wait(barrier, seq + 1)
    edge = pltpu.make_async_remote_copy(
        src_ref=streams.at[:, pl.ds(tokens - 16, 16), :],
        dst_ref=halo,
        send_sem=halo_sem.at[0],
        recv_sem=halo_sem.at[1],
        device_id={"seq": lax.rem(me + 1, seq)},
    )
    edge.start()
    for group in range(groups):
        send_all(send_filter, recv_filter, group, group)

    for slot in range(3):
        extended[slot, 16:, :] = streams[slot].astype(F32)
    edge.wait()
    keep = jnp.where(me > 0, 1.0, 0.0).astype(F32)
    for slot in range(3):
        extended[slot, :16, :] = halo[slot].astype(F32) * keep

    def short(slot, part, group):
        base = 16 + part * LANES
        at = lanes(group)
        return (
            taps_ref[0, slot:slot + 1, at] * extended[slot, base:base + LANES, at]
            + taps_ref[1, slot:slot + 1, at] * extended[slot, base - 1:base - 1 + LANES, at]
            + taps_ref[2, slot:slot + 1, at] * extended[slot, base - 2:base - 2 + LANES, at]
        )

    for group in range(groups):
        for part in range(sub):
            tile = short(1, part, group) * short(2, part, group)
            mixed[part * LANES:(part + 1) * LANES, lanes(group)] = tile
            scatter(tile.T, part)
        send_signal[group] = stage[...].astype(BF16)
        send_all(send_signal, recv_signal, group, groups + group)

    for group in range(groups):
        for part in range(sub):
            gate[part * LANES:(part + 1) * LANES, lanes(group)] = short(0, part, group)

    for load in loads[6:11]:
        load.wait()

    def transform(ref, group):
        stage[...] = ref[group].astype(F32)
        for pair in range(per // 2):
            values = jnp.concatenate(
                [stage[pl.ds(2 * pair + side, outer, stride=per), :] for side in range(2)], 1
            ).astype(BF16)
            outer_spec = dot(first[...], jnp.concatenate([values, values], 0))
            for side in range(2):
                real, imag = outer_spec[:outer, lanes(side)], outer_spec[outer:, lanes(side)]
                at = slice((2 * pair + side) * outer, (2 * pair + side + 1) * outer)
                high_ref[at, :LANES], low_ref[at, :LANES] = split(real * twist[0] + imag * twist[1])
                high_ref[at, LANES:], low_ref[at, LANES:] = split(imag * twist[0] - real * twist[1])
        return apply(forward)

    def apply(table):
        high, low = high_ref[...], low_ref[...]
        return dot(high, table[0]) + dot(low, table[0]) + dot(high, table[1])

    for group in range(groups):
        wait_all(recv_filter, group, recv_sem.at[group])
        spectrum[group] = transform(recv_filter, group)

    for group in range(groups):
        wait_all(recv_signal, group, recv_sem.at[groups + group])
        signal = transform(recv_signal, group)
        sig_real, sig_imag = signal[:, :LANES], signal[:, LANES:]
        fil_real, fil_imag = spectrum[group, :, :LANES], spectrum[group, :, LANES:]
        high_ref[:, :LANES], low_ref[:, :LANES] = split(sig_real * fil_real - sig_imag * fil_imag)
        high_ref[:, LANES:], low_ref[:, LANES:] = split(sig_real * fil_imag + sig_imag * fil_real)
        back = apply(backward)
        for pair in range(per // 2):
            sides = []
            for side in range(2):
                at = slice((2 * pair + side) * outer, (2 * pair + side + 1) * outer)
                real, imag = back[at, :LANES], back[at, LANES:]
                sides.append(jnp.concatenate(
                    [real * twist[0] - imag * twist[1], imag * twist[0] + real * twist[1]], 0
                ))
            high, low = split(jnp.concatenate(sides, 1))
            conv = dot(last[0], high) + dot(last[0], low) + dot(last[1], high)
            for side in range(2):
                stage[pl.ds(2 * pair + side, outer, stride=per), :] = conv[:, lanes(side)]
        send_conv[group] = stage[...].astype(BF16)
        send_all(send_conv, recv_conv, group, 2 * groups + group)

    half = tokens // 2
    hops = ((chan - 1) // 2, chan // 2)

    def hop(direction, step, group, side):
        origin = lax.rem(layer + (chan - step if direction == 0 else step), chan)
        piece = gathered.at[origin, group, pl.ds(side * half, half), :]
        return pltpu.make_async_remote_copy(
            src_ref=piece,
            dst_ref=piece,
            send_sem=ring_send.at[direction, step, group, side],
            recv_sem=ring_recv.at[direction, step, group, side],
            device_id={"chan": right if direction == 0 else left},
        )

    for group in range(groups):
        wait_all(recv_conv, group, recv_sem.at[2 * groups + group])
        stage[...] = recv_conv[group].astype(F32)
        for part in range(sub):
            conv = jnp.concatenate(
                [stage[pl.ds(part * per + channel, seq, stride=block), :] for channel in range(per)], 0
            ).T
            at = slice(part * LANES, (part + 1) * LANES)
            signal = mixed[at, lanes(group)]
            gated = gate[at, lanes(group)] * (conv + skip_ref[:, lanes(group)] * signal)
            gathered[layer, group, at, :] = gated.astype(BF16)
        for side in range(2):
            for direction in range(2):
                if hops[direction] > 0:
                    hop(direction, 0, group, side).start()

    loads[11].wait()

    def product(origin, side):
        at = slice(side * half, (side + 1) * half)
        values = jnp.concatenate([gathered[origin, group, at, :] for group in range(groups)], 1)
        depth = groups * LANES
        return dot(values, weight[pl.ds(pl.multiple_of(origin * depth, depth), depth), :])

    for side in range(2):
        total[side * half:(side + 1) * half, :] = product(layer, side)
    for step in range(1, chan // 2 + 1):
        final = step == chan // 2
        for direction in (1, 0):
            if step > hops[direction]:
                continue
            origin = lax.rem(layer + (chan - step if direction == 0 else step), chan)
            for side in range(2):
                at = slice(side * half, (side + 1) * half)
                for group in range(groups):
                    hop(direction, step - 1, group, side).wait_recv()
                    if step < hops[direction]:
                        hop(direction, step, group, side).start()
                if final:
                    out_ref[at, :] = (total[at, :] + product(origin, side)).astype(BF16)
        if not final:
            for direction in (1, 0):
                if step <= hops[direction]:
                    origin = lax.rem(layer + (chan - step if direction == 0 else step), chan)
                    for side in range(2):
                        total[side * half:(side + 1) * half, :] += product(origin, side)

    for group in range(groups):
        for slot, ref in enumerate((send_filter, send_signal, send_conv)):
            wait_all(ref, group, send_sem.at[slot * groups + group])
    for group in range(groups):
        for side in range(2):
            for direction in range(2):
                for step in range(hops[direction]):
                    hop(direction, step, group, side).wait_send()


def shards(query_proj, key_proj, value_proj, short_taps, kernel, skip, out_weight):
    seq, chan = lax.axis_size("seq"), lax.axis_size("chan")
    tokens, width = query_proj.shape
    groups = width // LANES
    per = LANES // seq
    outer = seq * tokens // LANES
    rows = outer * per
    features = out_weight.shape[1]
    tables = build_tables(outer)
    anywhere = pl.BlockSpec(memory_space=pl.ANY)
    inside = pl.BlockSpec(memory_space=pltpu.VMEM)
    exchange = pltpu.VMEM((groups, rows, LANES), BF16)
    return pl.pallas_call(
        functools.partial(operator, GRIDS[seq], seq, chan),
        out_shape=pltpu.VMEM((tokens, features), BF16),
        in_specs=[anywhere] * 12,
        out_specs=inside,
        scratch_shapes=[
            pltpu.VMEM((3, tokens, width), BF16),
            pltpu.VMEM((3, 16, width), BF16),
            pltpu.VMEM((tokens, width), F32),
            pltpu.VMEM(short_taps.shape, F32),
            pltpu.VMEM((1, width), F32),
            pltpu.VMEM(out_weight.shape, BF16),
            *(pltpu.VMEM(table.shape, table.dtype) for table in tables),
            pltpu.VMEM((3, tokens + 16, width), F32),
            pltpu.VMEM((tokens, width), F32),
            pltpu.VMEM((tokens, width), F32),
            pltpu.VMEM((rows, LANES), F32),
            exchange, exchange, exchange, exchange, exchange, exchange,
            pltpu.VMEM((groups, rows, 2 * LANES), F32),
            pltpu.VMEM((rows, 2 * LANES), BF16),
            pltpu.VMEM((rows, 2 * LANES), BF16),
            pltpu.VMEM((chan, groups, tokens, LANES), BF16),
            pltpu.VMEM((tokens, features), F32),
            pltpu.SemaphoreType.DMA((12,)),
            pltpu.SemaphoreType.DMA((2,)),
            pltpu.SemaphoreType.DMA((3 * groups,)),
            pltpu.SemaphoreType.DMA((3 * groups,)),
            pltpu.SemaphoreType.DMA((2, max(1, chan // 2), groups, 2)),
            pltpu.SemaphoreType.DMA((2, max(1, chan // 2), groups, 2)),
        ],
        compiler_params=pltpu.CompilerParams(
            collective_id=0, has_side_effects=True, vmem_limit_bytes=56 * 1024 * 1024
        ),
        cost_estimate=pl.CostEstimate(flops=2_000_000_000, bytes_accessed=5_000_000, transcendentals=0),
    )(
        query_proj, key_proj, value_proj, short_taps, kernel, skip.reshape(1, width), out_weight,
        *(jnp.asarray(table) for table in tables),
    )


def solution(mesh):
    return jax.shard_map(
        shards,
        mesh=mesh,
        in_specs=(
            P("seq", "chan"),
            P("seq", "chan"),
            P("seq", "chan"),
            P(None, None, "chan"),
            P("seq", "chan"),
            P("chan"),
            P(None, "chan"),
        ),
        out_specs=P("seq", "chan"),
        check_vma=False,
    )
```

```python
import functools
import math

import jax
import jax.numpy as jnp
import ml_dtypes
import numpy as np
from jax import lax
from jax.experimental import pallas as pl
from jax.experimental.pallas import tpu as pltpu
from jax.sharding import PartitionSpec as P

LANES = 128
F32 = jnp.float32
BF16 = jnp.bfloat16
RIGHTWARD, LEFTWARD_LAYER = (0,), 0
GRIDS = {32: (4, 4, 2), 8: (2, 2, 2), 4: (1, 2, 2)}


def high_low(table):
    high = table.astype(ml_dtypes.bfloat16)
    low = (table - high.astype(np.float64)).astype(ml_dtypes.bfloat16)
    return high, low


def build_tables(outer):
    length = outer * LANES
    position = np.arange(outer)
    lane = np.arange(LANES)
    angle = 2.0 * math.pi / (4 * outer) * ((4 * position[:, None] + 1) * position[None, :] % (4 * outer))
    first = np.concatenate([np.cos(angle), -np.sin(angle)], 0)
    last = np.concatenate([np.cos(angle).T, -np.sin(angle).T], 1) / length
    twist = 2.0 * math.pi / (4 * length) * ((4 * position[:, None] + 1) * lane[None, :] % (4 * length))
    inner = 2.0 * math.pi / LANES * (lane[:, None] * lane[None, :] % LANES)
    cos, sin = np.cos(inner), np.sin(inner)
    forward = np.block([[cos, -sin], [sin, cos]])
    backward = np.block([[cos, sin], [-sin, cos]])
    return (
        np.concatenate(high_low(first), 1),
        np.stack([np.cos(twist), np.sin(twist)]).astype(np.float32),
        np.stack(high_low(forward)),
        np.stack(high_low(backward)),
        np.stack(high_low(last)),
    )


def split(values):
    high = values.astype(BF16)
    return high, (values - high.astype(F32)).astype(BF16)


def dot(lhs, rhs):
    return jnp.dot(lhs, rhs, preferred_element_type=F32)


def peers(me, grid):
    along_x, along_y, cores = grid
    x, y, core = me // (along_y * cores), me // cores % along_y, me % cores
    steps = [(i, j, k) for i in range(along_x) for j in range(along_y) for k in range(cores)][1:]
    steps.sort(key=lambda step: -4 * (min(step[0], along_x - step[0]) + min(step[1], along_y - step[1])) - step[2])
    return [
        ((x + i) % along_x * along_y + (y + j) % along_y) * cores + (core + k) % cores
        for i, j, k in steps
    ]


def operator(
    grid, seq, chan,
    query_hbm, key_hbm, value_hbm, taps_hbm, filter_hbm, skip_hbm, weight_hbm,
    first_hbm, twist_hbm, forward_hbm, backward_hbm, last_hbm,
    out_ref,
    streams, halo, filt, taps_ref, skip_ref, weight, first, twist, forward, backward, last,
    extended, mixed, gate, stage, edges, send_edge, recv_edge, send_in, recv_in, send_conv, recv_conv,
    spectrum, high_ref, low_ref, gathered, total,
    load_sem, halo_sem, send_sem, recv_sem, ring_send, ring_recv,
):
    me = lax.axis_index("seq")
    layer = lax.axis_index("chan")
    tokens = streams.shape[1]
    sub = tokens // LANES
    outer = seq * sub
    width = streams.shape[2]
    groups = width // LANES
    per = LANES // seq
    block = sub * per
    rows = seq * block

    loads = [
        pltpu.make_async_copy(source, target, load_sem.at[slot])
        for slot, (source, target) in enumerate((
            (filter_hbm, filt),
            (key_hbm, streams.at[1]),
            (value_hbm, streams.at[2]),
            (query_hbm, streams.at[0]),
            (taps_hbm, taps_ref),
            (skip_hbm, skip_ref),
            (first_hbm, first),
            (twist_hbm, twist),
            (forward_hbm, forward),
            (backward_hbm, backward),
            (last_hbm, last),
            (weight_hbm, weight),
        ))
    ]
    barrier = pltpu.get_barrier_semaphore()

    others = peers(me, grid)
    for other in others:
        pl.semaphore_signal(barrier, inc=1, device_id={"seq": other})
    right = lax.rem(layer + 1, chan)
    left = lax.rem(layer + chan - 1, chan)
    pl.semaphore_signal(barrier, inc=1, device_id={"chan": right})
    pl.semaphore_signal(barrier, inc=1, device_id={"chan": left})
    for load in loads:
        load.start()

    def lanes(group):
        return slice(group * LANES, (group + 1) * LANES)

    def scatter(tile, part):
        for channel in range(per):
            stage[pl.ds(part * per + channel, seq, stride=block), :] = tile[channel * seq:(channel + 1) * seq, :]

    def staged():
        return stage[...].astype(BF16).reshape(seq, block, LANES)

    def send_all(source, target, slot):
        for other in others:
            pltpu.make_async_remote_copy(
                src_ref=source.at[other],
                dst_ref=target.at[me],
                send_sem=send_sem.at[slot],
                recv_sem=recv_sem.at[slot],
                device_id={"seq": other},
            ).start()
        target[me] = source[me]

    def wait_all(ref, sem):
        part = ref.at[pl.ds(0, seq - 1)]
        pltpu.make_async_copy(part, part, sem).wait()

    def short(slot, group, base=0, count=LANES):
        at = lanes(group)
        base += 16
        return (
            taps_ref[0, slot:slot + 1, at] * extended[slot, base:base + count, at]
            + taps_ref[1, slot:slot + 1, at] * extended[slot, base - 1:base - 1 + count, at]
            + taps_ref[2, slot:slot + 1, at] * extended[slot, base - 2:base - 2 + count, at]
        )

    def prepare(group):
        for part in range(sub):
            scatter(filt[part * LANES:(part + 1) * LANES, lanes(group)].T, part)
        send_in[group, 0] = staged()
        for part in range(sub):
            tile = short(1, group, part * LANES) * short(2, group, part * LANES)
            mixed[part * LANES:(part + 1) * LANES, lanes(group)] = tile
            scatter(tile.T, part)
        send_in[group, 1] = staged()

    loads[4].wait()
    for slot in (1, 2):
        loads[slot].wait()
        extended[slot, 8:16, :] = jnp.zeros((8, width), F32)
        extended[slot, 16:, :] = streams[slot].astype(F32)

    parts = []
    for begin in (True, False):
        for slot in (1, 2):
            tap = [taps_ref[shift, slot:slot + 1, :] for shift in range(3)]
            if begin:
                head = [extended[slot, 16 + row:17 + row, :] for row in range(2)]
                parts += [tap[0] * head[0], tap[0] * head[1] + tap[1] * head[0]]
            else:
                tail = [extended[slot, 14 + tokens + row:15 + tokens + row, :] for row in range(2)]
                parts += [tap[1] * tail[1] + tap[2] * tail[0], tap[2] * tail[1]]
    parts = jnp.concatenate(parts, 0)
    edges[...] = jnp.zeros(edges.shape, F32)
    for group in range(groups):
        for channel in range(per):
            at = (group * per + channel) * 8
            edges[at:at + 8, :] = pltpu.roll(parts[:, lanes(group)], (LANES - channel * seq) % LANES, 1)
    by_holder = edges[...].T
    for holder in range(seq):
        send_edge[holder] = by_holder[holder:holder + 1, :]

    loads[0].wait()
    prepare(0)
    pl.semaphore_wait(barrier, seq + 1)
    for which in range(2):
        send_all(send_in.at[0, which], recv_in.at[0, which], which)
    send_all(send_edge, recv_edge, 2 * groups)
    for group in range(1, groups):
        prepare(group)
        for which in range(2):
            send_all(send_in.at[group, which], recv_in.at[group, which], 2 * group + which)
    loads[3].wait()
    edge = pltpu.make_async_remote_copy(
        src_ref=streams.at[:, pl.ds(tokens - 16, 16), :],
        dst_ref=halo,
        send_sem=halo_sem.at[0],
        recv_sem=halo_sem.at[1],
        device_id={"seq": lax.rem(me + 1, seq)},
    )
    edge.start()
    extended[0, 16:, :] = streams[0].astype(F32)
    for load in loads[5:11]:
        load.wait()

    def apply(table):
        high, low = high_ref[...], low_ref[...]
        return dot(high, table[0]) + dot(low, table[0]) + dot(high, table[1])

    def transform(group, which):
        stage[...] = recv_in[group, which].reshape(rows, LANES).astype(F32)
        if which == 1:
            first_lanes = lax.broadcasted_iota(jnp.int32, (seq, LANES), 1) < 2
            for channel in range(per):
                at = pl.ds(channel, seq, stride=block)
                place = (group * per + channel) * 8
                whole = pltpu.roll(heads, (wide - place) % wide, 1)[:, :LANES]
                stage[at, :] = jnp.where(first_lanes, whole, stage[at, :])
        for pair in range(per // 2):
            values = jnp.concatenate(
                [stage[pl.ds(2 * pair + side, outer, stride=per), :] for side in range(2)], 1
            ).astype(BF16)
            outer_spec = dot(first[...], jnp.concatenate([values, values], 0))
            for side in range(2):
                real, imag = outer_spec[:outer, lanes(side)], outer_spec[outer:, lanes(side)]
                at = slice((2 * pair + side) * outer, (2 * pair + side + 1) * outer)
                high_ref[at, :LANES], low_ref[at, :LANES] = split(real * twist[0] + imag * twist[1])
                high_ref[at, LANES:], low_ref[at, LANES:] = split(imag * twist[0] - real * twist[1])
        spectrum[which * rows:(which + 1) * rows, :] = apply(forward)

    for group in range(groups):
        wait_all(recv_in.at[group, 0], recv_sem.at[2 * group])
        transform(group, 0)
        wait_all(recv_in.at[group, 1], recv_sem.at[2 * group + 1])
        if group == 0:
            wait_all(recv_edge, recv_sem.at[2 * groups])
            own = jnp.concatenate([recv_edge[holder] for holder in range(seq)], 0)
            wide = own.shape[1]
            first_row = lax.broadcasted_iota(jnp.int32, own.shape, 0) < 1
            carried = jnp.where(first_row, 0.0, pltpu.roll(own, 1, 0))
            short_heads = own + pltpu.roll(carried, wide - 4, 1)
            heads = short_heads * pltpu.roll(short_heads, wide - 2, 1)
        transform(group, 1)
        fil_real, fil_imag = spectrum[:rows, :LANES], spectrum[:rows, LANES:]
        sig_real, sig_imag = spectrum[rows:, :LANES], spectrum[rows:, LANES:]
        high_ref[:, :LANES], low_ref[:, :LANES] = split(sig_real * fil_real - sig_imag * fil_imag)
        high_ref[:, LANES:], low_ref[:, LANES:] = split(sig_real * fil_imag + sig_imag * fil_real)
        back = apply(backward)
        for pair in range(per // 2):
            sides = []
            for side in range(2):
                at = slice((2 * pair + side) * outer, (2 * pair + side + 1) * outer)
                real, imag = back[at, :LANES], back[at, LANES:]
                sides.append(jnp.concatenate(
                    [real * twist[0] - imag * twist[1], imag * twist[0] + real * twist[1]], 0
                ))
            high, low = split(jnp.concatenate(sides, 1))
            conv = dot(last[0], high) + dot(last[0], low) + dot(last[1], high)
            for side in range(2):
                stage[pl.ds(2 * pair + side, outer, stride=per), :] = conv[:, lanes(side)]
        send_conv[group] = staged()
        send_all(send_conv.at[group], recv_conv.at[group], 2 * groups + 1 + group)

    edge.wait()
    keep = jnp.where(me > 0, 1.0, 0.0).astype(F32)
    for slot in range(3):
        extended[slot, :16, :] = halo[slot].astype(F32) * keep
    for group in range(groups):
        mixed[:8, lanes(group)] = short(1, group, 0, 8) * short(2, group, 0, 8)
        for part in range(sub):
            gate[part * LANES:(part + 1) * LANES, lanes(group)] = short(0, group, part * LANES)

    farthest = chan // 2

    def hop(direction, step, group):
        origin = lax.rem(layer + (chan - step if direction == 0 else step), chan)
        piece = gathered.at[origin, group]
        return pltpu.make_async_remote_copy(
            src_ref=piece,
            dst_ref=piece,
            send_sem=ring_send.at[direction, step, group],
            recv_sem=ring_recv.at[direction, step, group],
            device_id={"chan": right if direction == 0 else left},
        )

    def if_used(direction, step, group, target, act):
        if step < farthest - 1:
            act()
        elif group in RIGHTWARD:
            pl.when(target != LEFTWARD_LAYER if direction == 0 else target == LEFTWARD_LAYER)(act)
        elif direction == 1:
            act()

    def pass_on(direction, step, group):
        if_used(direction, step, group, right if direction == 0 else left, lambda: hop(direction, step, group).start())

    for group in range(groups):
        wait_all(recv_conv.at[group], recv_sem.at[2 * groups + 1 + group])
        stage[...] = recv_conv[group].reshape(rows, LANES).astype(F32)
        for part in range(sub):
            conv = jnp.concatenate(
                [stage[pl.ds(part * per + channel, seq, stride=block), :] for channel in range(per)], 0
            ).T
            at = slice(part * LANES, (part + 1) * LANES)
            signal = mixed[at, lanes(group)]
            gated = gate[at, lanes(group)] * (conv + skip_ref[:, lanes(group)] * signal)
            gathered[layer, group, at, :] = gated.astype(BF16)
        for direction in (1, 0):
            pass_on(direction, 0, group)

    loads[11].wait()

    def product(origin, begin, count, members=tuple(range(groups))):
        values = jnp.concatenate([gathered[origin, group, begin:begin + count, :] for group in members], 1)
        depth = groups * LANES
        at = pl.ds(pl.multiple_of(origin * depth + members[0] * LANES, LANES), len(members) * LANES)
        return dot(values, weight[at, :])

    def origin_of(direction, step):
        return lax.rem(layer + (chan - step if direction == 0 else step), chan)

    half = tokens // 2
    for begin in (0, half):
        total[begin:begin + half, :] = product(layer, begin, half)
    for step in range(1, farthest + 1):
        for group in range(groups):
            for direction in (1, 0):
                if_used(direction, step - 1, group, layer, lambda: hop(direction, step - 1, group).wait_recv())
                if step < farthest:
                    pass_on(direction, step, group)
            if step == farthest:
                for begin in (0, half):
                    at = slice(begin, begin + half)
                    value = total[at, :] + product(origin_of(1, step), begin, half, (group,))
                    if group < groups - 1:
                        total[at, :] = value
                    else:
                        out_ref[at, :] = value.astype(BF16)
        if step < farthest:
            for direction in (1, 0):
                for begin in (0, half):
                    total[begin:begin + half, :] += product(origin_of(direction, step), begin, half)

    wait_all(send_edge, send_sem.at[2 * groups])
    for group in range(groups):
        for which in range(2):
            wait_all(send_in.at[group, which], send_sem.at[2 * group + which])
        wait_all(send_conv.at[group], send_sem.at[2 * groups + 1 + group])
        for direction in range(2):
            for step in range(farthest):
                if_used(
                    direction, step, group, right if direction == 0 else left,
                    lambda: hop(direction, step, group).wait_send(),
                )


def shards(query_proj, key_proj, value_proj, short_taps, kernel, skip, out_weight):
    seq, chan = lax.axis_size("seq"), lax.axis_size("chan")
    tokens, width = query_proj.shape
    groups = width // LANES
    per = LANES // seq
    outer = seq * tokens // LANES
    rows = outer * per
    features = out_weight.shape[1]
    tables = build_tables(outer)
    anywhere = pl.BlockSpec(memory_space=pl.ANY)
    inside = pl.BlockSpec(memory_space=pltpu.VMEM)
    block = rows // seq
    wide = -(-groups * per * 8 // LANES) * LANES
    incoming = pltpu.VMEM((groups, 2, seq, block, LANES), BF16)
    returned = pltpu.VMEM((groups, seq, block, LANES), BF16)
    edge = pltpu.VMEM((seq, 1, wide), F32)
    return pl.pallas_call(
        functools.partial(operator, GRIDS[seq], seq, chan),
        out_shape=pltpu.VMEM((tokens, features), BF16),
        in_specs=[anywhere] * 12,
        out_specs=inside,
        scratch_shapes=[
            pltpu.VMEM((3, tokens, width), BF16),
            pltpu.VMEM((3, 16, width), BF16),
            pltpu.VMEM((tokens, width), F32),
            pltpu.VMEM(short_taps.shape, F32),
            pltpu.VMEM((1, width), F32),
            pltpu.VMEM(out_weight.shape, BF16),
            *(pltpu.VMEM(table.shape, table.dtype) for table in tables),
            pltpu.VMEM((3, tokens + 16, width), F32),
            pltpu.VMEM((tokens, width), F32),
            pltpu.VMEM((tokens, width), F32),
            pltpu.VMEM((rows, LANES), F32),
            pltpu.VMEM((wide, LANES), F32),
            edge, edge, incoming, incoming, returned, returned,
            pltpu.VMEM((2 * rows, 2 * LANES), F32),
            pltpu.VMEM((rows, 2 * LANES), BF16),
            pltpu.VMEM((rows, 2 * LANES), BF16),
            pltpu.VMEM((chan, groups, tokens, LANES), BF16),
            pltpu.VMEM((tokens, features), F32),
            pltpu.SemaphoreType.DMA((12,)),
            pltpu.SemaphoreType.DMA((2,)),
            pltpu.SemaphoreType.DMA((3 * groups + 1,)),
            pltpu.SemaphoreType.DMA((3 * groups + 1,)),
            pltpu.SemaphoreType.DMA((2, max(1, chan // 2), groups)),
            pltpu.SemaphoreType.DMA((2, max(1, chan // 2), groups)),
        ],
        compiler_params=pltpu.CompilerParams(
            collective_id=0, has_side_effects=True, vmem_limit_bytes=56 * 1024 * 1024
        ),
        cost_estimate=pl.CostEstimate(flops=2_000_000_000, bytes_accessed=5_000_000, transcendentals=0),
    )(
        query_proj, key_proj, value_proj, short_taps, kernel, skip.reshape(1, width), out_weight,
        *(jnp.asarray(table) for table in tables),
    )


def solution(mesh):
    return jax.shard_map(
        shards,
        mesh=mesh,
        in_specs=(
            P("seq", "chan"),
            P("seq", "chan"),
            P("seq", "chan"),
            P(None, None, "chan"),
            P("seq", "chan"),
            P("chan"),
            P(None, "chan"),
        ),
        out_specs=P("seq", "chan"),
        check_vma=False,
    )
```

```python
import functools
import math

import jax
import jax.numpy as jnp
import ml_dtypes
import numpy as np
from jax import lax
from jax.experimental import pallas as pl
from jax.experimental.pallas import tpu as pltpu
from jax.sharding import PartitionSpec as P

LANES = 128
F32 = jnp.float32
BF16 = jnp.bfloat16
RIGHTWARD, LEFTWARD_LAYERS = (1,), (0, 1)
GRIDS = {32: (4, 4, 2), 8: (2, 2, 2), 4: (1, 2, 2)}


def high_low(table):
    high = table.astype(ml_dtypes.bfloat16)
    low = (table - high.astype(np.float64)).astype(ml_dtypes.bfloat16)
    return high, low


def build_tables(outer):
    length = outer * LANES
    position = np.arange(outer)
    lane = np.arange(LANES)
    angle = 2.0 * math.pi / (4 * outer) * ((4 * position[:, None] + 1) * position[None, :] % (4 * outer))
    first = np.concatenate([np.cos(angle), -np.sin(angle)], 0)
    last = np.concatenate([np.cos(angle).T, -np.sin(angle).T], 1) / length
    twist = 2.0 * math.pi / (4 * length) * ((4 * position[:, None] + 1) * lane[None, :] % (4 * length))
    inner = 2.0 * math.pi / LANES * (lane[:, None] * lane[None, :] % LANES)
    cos, sin = np.cos(inner), np.sin(inner)
    forward = np.block([[cos, -sin], [sin, cos]])
    backward = np.block([[cos, sin], [-sin, cos]])
    return (
        np.concatenate(high_low(first), 1),
        np.stack([np.cos(twist), np.sin(twist)]).astype(np.float32),
        np.stack(high_low(forward)),
        np.stack(high_low(backward)),
        np.stack(high_low(last)),
    )


def split(values):
    high = values.astype(BF16)
    return high, (values - high.astype(F32)).astype(BF16)


def dot(lhs, rhs):
    return jnp.dot(lhs, rhs, preferred_element_type=F32)


def peers(me, grid):
    along_x, along_y, cores = grid
    x, y, core = me // (along_y * cores), me // cores % along_y, me % cores
    steps = [(i, j, k) for i in range(along_x) for j in range(along_y) for k in range(cores)][1:]
    steps.sort(key=lambda step: -4 * (min(step[0], along_x - step[0]) + min(step[1], along_y - step[1])) - step[2])
    return [
        ((x + i) % along_x * along_y + (y + j) % along_y) * cores + (core + k) % cores
        for i, j, k in steps
    ]


def operator(
    grid, seq, chan,
    query_hbm, key_hbm, value_hbm, taps_hbm, filter_hbm, skip_hbm, weight_hbm,
    first_hbm, twist_hbm, forward_hbm, backward_hbm, last_hbm,
    out_ref,
    streams, halo, filt, taps_ref, skip_ref, weight, first, twist, forward, backward, last,
    extended, mixed, gate, stage, edges, send_edge, recv_edge, send_in, recv_in, send_conv, recv_conv,
    spectrum, high_ref, low_ref, gathered, total,
    load_sem, halo_sem, send_sem, recv_sem, ring_send, ring_recv,
):
    me = lax.axis_index("seq")
    layer = lax.axis_index("chan")
    tokens = streams.shape[1]
    sub = tokens // LANES
    outer = seq * sub
    width = streams.shape[2]
    groups = width // LANES
    per = LANES // seq
    block = sub * per
    rows = seq * block

    loads = [
        pltpu.make_async_copy(source, target, load_sem.at[slot])
        for slot, (source, target) in enumerate((
            (filter_hbm, filt),
            (key_hbm, streams.at[1]),
            (value_hbm, streams.at[2]),
            (query_hbm, streams.at[0]),
            (taps_hbm, taps_ref),
            (skip_hbm, skip_ref),
            (first_hbm, first),
            (twist_hbm, twist),
            (forward_hbm, forward),
            (backward_hbm, backward),
            (last_hbm, last),
            (weight_hbm, weight),
        ))
    ]
    barrier = pltpu.get_barrier_semaphore()

    others = peers(me, grid)
    for other in others:
        pl.semaphore_signal(barrier, inc=1, device_id={"seq": other})
    right = lax.rem(layer + 1, chan)
    left = lax.rem(layer + chan - 1, chan)
    pl.semaphore_signal(barrier, inc=1, device_id={"chan": right})
    pl.semaphore_signal(barrier, inc=1, device_id={"chan": left})
    for load in loads:
        load.start()

    def lanes(group):
        return slice(group * LANES, (group + 1) * LANES)

    def scatter(tile, part):
        for channel in range(per):
            stage[pl.ds(part * per + channel, seq, stride=block), :] = tile[channel * seq:(channel + 1) * seq, :]

    def staged():
        return stage[:rows, :].astype(BF16).reshape(seq, block, LANES)

    def send_all(source, target, slot):
        for other in others:
            pltpu.make_async_remote_copy(
                src_ref=source.at[other],
                dst_ref=target.at[me],
                send_sem=send_sem.at[slot],
                recv_sem=recv_sem.at[slot],
                device_id={"seq": other},
            ).start()
        target[me] = source[me]

    def wait_all(ref, sem):
        part = ref.at[pl.ds(0, seq - 1)]
        pltpu.make_async_copy(part, part, sem).wait()

    def short(slot, group, base=0, count=LANES):
        at = lanes(group)
        base += 16
        return (
            taps_ref[0, slot:slot + 1, at] * extended[slot, base:base + count, at]
            + taps_ref[1, slot:slot + 1, at] * extended[slot, base - 1:base - 1 + count, at]
            + taps_ref[2, slot:slot + 1, at] * extended[slot, base - 2:base - 2 + count, at]
        )

    def prepare(group):
        for part in range(sub):
            scatter(filt[part * LANES:(part + 1) * LANES, lanes(group)].T, part)
        send_in[group, 0] = staged()
        for part in range(sub):
            tile = short(1, group, part * LANES) * short(2, group, part * LANES)
            mixed[part * LANES:(part + 1) * LANES, lanes(group)] = tile
            scatter(tile.T, part)
        send_in[group, 1] = staged()

    loads[4].wait()
    for slot in (1, 2):
        loads[slot].wait()
        extended[slot, 8:16, :] = jnp.zeros((8, width), F32)
        extended[slot, 16:, :] = streams[slot].astype(F32)

    parts = []
    for begin in (True, False):
        for slot in (1, 2):
            tap = [taps_ref[shift, slot:slot + 1, :] for shift in range(3)]
            if begin:
                head = [extended[slot, 16 + row:17 + row, :] for row in range(2)]
                parts += [tap[0] * head[0], tap[0] * head[1] + tap[1] * head[0]]
            else:
                tail = [extended[slot, 14 + tokens + row:15 + tokens + row, :] for row in range(2)]
                parts += [tap[1] * tail[1] + tap[2] * tail[0], tap[2] * tail[1]]
    parts = jnp.concatenate(parts, 0)
    edges[...] = jnp.zeros(edges.shape, F32)
    for group in range(groups):
        for channel in range(per):
            at = (group * per + channel) * 8
            edges[at:at + 8, :] = pltpu.roll(parts[:, lanes(group)], (LANES - channel * seq) % LANES, 1)
    by_holder = edges[...].T
    for holder in range(seq):
        send_edge[holder] = by_holder[holder:holder + 1, :]

    loads[0].wait()
    prepare(0)
    pl.semaphore_wait(barrier, seq + 1)
    send_all(send_in.at[0, 0], recv_in.at[0, 0], 0)
    send_all(send_edge, recv_edge, 2 * groups)
    send_all(send_in.at[0, 1], recv_in.at[0, 1], 1)
    for group in range(1, groups):
        prepare(group)
        for which in range(2):
            send_all(send_in.at[group, which], recv_in.at[group, which], 2 * group + which)
    loads[3].wait()
    edge = pltpu.make_async_remote_copy(
        src_ref=streams.at[:, pl.ds(tokens - 16, 16), :],
        dst_ref=halo,
        send_sem=halo_sem.at[0],
        recv_sem=halo_sem.at[1],
        device_id={"seq": lax.rem(me + 1, seq)},
    )
    edge.start()
    extended[0, 16:, :] = streams[0].astype(F32)
    for load in loads[5:11]:
        load.wait()

    def apply(table):
        high, low = high_ref[...], low_ref[...]
        return dot(high, table[0]) + dot(low, table[0]) + dot(high, table[1])

    def transform(group, which):
        stage[:rows, :] = recv_in[group, which].reshape(rows, LANES).astype(F32)
        if which == 1:
            first_lanes = lax.broadcasted_iota(jnp.int32, (seq, LANES), 1) < 2
            for channel in range(per):
                at = pl.ds(channel, seq, stride=block)
                place = (group * per + channel) * 8
                whole = pltpu.roll(heads, (wide - place) % wide, 1)[:, :LANES]
                stage[at, :] = jnp.where(first_lanes, whole, stage[at, :])
        values = jnp.concatenate([stage[pl.ds(channel, outer, stride=per), :] for channel in range(per)], 1).astype(BF16)
        outer_spec = dot(first[...], jnp.concatenate([values, values], 0))
        for channel in range(per):
            real, imag = outer_spec[:outer, lanes(channel)], outer_spec[outer:, lanes(channel)]
            at = slice(channel * outer, (channel + 1) * outer)
            high_ref[at, :LANES], low_ref[at, :LANES] = split(real * twist[0] + imag * twist[1])
            high_ref[at, LANES:], low_ref[at, LANES:] = split(imag * twist[0] - real * twist[1])
        spectrum[which * rows:(which + 1) * rows, :] = apply(forward)

    for group in range(groups):
        wait_all(recv_in.at[group, 0], recv_sem.at[2 * group])
        transform(group, 0)
        wait_all(recv_in.at[group, 1], recv_sem.at[2 * group + 1])
        if group == 0:
            wait_all(recv_edge, recv_sem.at[2 * groups])
            own = jnp.concatenate([recv_edge[holder] for holder in range(seq)], 0)
            wide = own.shape[1]
            first_row = lax.broadcasted_iota(jnp.int32, own.shape, 0) < 1
            carried = jnp.where(first_row, 0.0, pltpu.roll(own, 1, 0))
            short_heads = own + pltpu.roll(carried, wide - 4, 1)
            heads = short_heads * pltpu.roll(short_heads, wide - 2, 1)
        transform(group, 1)
        fil_real, fil_imag = spectrum[:rows, :LANES], spectrum[:rows, LANES:]
        sig_real, sig_imag = spectrum[rows:, :LANES], spectrum[rows:, LANES:]
        high_ref[:, :LANES], low_ref[:, :LANES] = split(sig_real * fil_real - sig_imag * fil_imag)
        high_ref[:, LANES:], low_ref[:, LANES:] = split(sig_real * fil_imag + sig_imag * fil_real)
        back = apply(backward)
        for pair in range(per // 2):
            sides = []
            for side in range(2):
                at = slice((2 * pair + side) * outer, (2 * pair + side + 1) * outer)
                real, imag = back[at, :LANES], back[at, LANES:]
                sides.append(jnp.concatenate(
                    [real * twist[0] - imag * twist[1], imag * twist[0] + real * twist[1]], 0
                ))
            high, low = split(jnp.concatenate(sides, 1))
            both = dot(last[...].reshape(2 * outer, 2 * outer), high)
            conv = both[:outer] + both[outer:] + dot(last[0], low)
            for side in range(2):
                stage[pl.ds(2 * pair + side, outer, stride=per), :] = conv[:, lanes(side)]
        send_conv[group] = staged()
        send_all(send_conv.at[group], recv_conv.at[group], 2 * groups + 1 + group)

    edge.wait()
    keep = jnp.where(me > 0, 1.0, 0.0).astype(F32)
    for slot in range(3):
        extended[slot, :16, :] = halo[slot].astype(F32) * keep
    for group in range(groups):
        mixed[:8, lanes(group)] = short(1, group, 0, 8) * short(2, group, 0, 8)
        for part in range(sub):
            gate[part * LANES:(part + 1) * LANES, lanes(group)] = short(0, group, part * LANES)

    farthest = chan // 2

    def hop(direction, step, group):
        origin = lax.rem(layer + (chan - step if direction == 0 else step), chan)
        piece = gathered.at[origin, group]
        return pltpu.make_async_remote_copy(
            src_ref=piece,
            dst_ref=piece,
            send_sem=ring_send.at[direction, step, group],
            recv_sem=ring_recv.at[direction, step, group],
            device_id={"chan": right if direction == 0 else left},
        )

    def if_used(direction, step, group, target, act):
        if step < farthest - 1:
            act()
        elif group in RIGHTWARD:
            by_left = functools.reduce(jnp.logical_or, [target == other for other in LEFTWARD_LAYERS])
            pl.when(by_left if direction == 1 else jnp.logical_not(by_left))(act)
        elif direction == 1:
            act()

    def pass_on(direction, step, group):
        if_used(direction, step, group, right if direction == 0 else left, lambda: hop(direction, step, group).start())

    for group in range(groups):
        wait_all(recv_conv.at[group], recv_sem.at[2 * groups + 1 + group])
        stage[:rows, :] = recv_conv[group].reshape(rows, LANES).astype(F32)
        for part in range(sub):
            conv = jnp.concatenate(
                [stage[pl.ds(part * per + channel, seq, stride=block), :] for channel in range(per)], 0
            ).T
            at = slice(part * LANES, (part + 1) * LANES)
            signal = mixed[at, lanes(group)]
            gated = gate[at, lanes(group)] * (conv + skip_ref[:, lanes(group)] * signal)
            gathered[layer, group, at, :] = gated.astype(BF16)
        for direction in (1, 0):
            pass_on(direction, 0, group)

    loads[11].wait()

    def product(origin, begin, count, members=tuple(range(groups))):
        values = jnp.concatenate([gathered[origin, group, begin:begin + count, :] for group in members], 1)
        depth = groups * LANES
        at = pl.ds(pl.multiple_of(origin * depth + members[0] * LANES, LANES), len(members) * LANES)
        return dot(values, weight[at, :])

    def origin_of(direction, step):
        return lax.rem(layer + (chan - step if direction == 0 else step), chan)

    half = tokens // 2
    for begin in (0, half):
        total[begin:begin + half, :] = product(layer, begin, half)
    for step in range(1, farthest + 1):
        for group in range(groups):
            for direction in (1, 0):
                if_used(direction, step - 1, group, layer, lambda: hop(direction, step - 1, group).wait_recv())
                if step < farthest:
                    pass_on(direction, step, group)
            if step == farthest:
                for begin in (0, half):
                    at = slice(begin, begin + half)
                    if group == groups - 1:
                        out_ref[at, :] = (total[at, :] + product(origin_of(1, step), begin, half)).astype(BF16)
        if step < farthest:
            for direction in (1, 0):
                for begin in (0, half):
                    total[begin:begin + half, :] += product(origin_of(direction, step), begin, half)

    wait_all(send_edge, send_sem.at[2 * groups])
    for group in range(groups):
        for which in range(2):
            wait_all(send_in.at[group, which], send_sem.at[2 * group + which])
        wait_all(send_conv.at[group], send_sem.at[2 * groups + 1 + group])
        for direction in range(2):
            for step in range(farthest):
                if_used(
                    direction, step, group, right if direction == 0 else left,
                    lambda: hop(direction, step, group).wait_send(),
                )


def shards(query_proj, key_proj, value_proj, short_taps, kernel, skip, out_weight):
    seq, chan = lax.axis_size("seq"), lax.axis_size("chan")
    tokens, width = query_proj.shape
    groups = width // LANES
    per = LANES // seq
    outer = seq * tokens // LANES
    rows = outer * per
    features = out_weight.shape[1]
    tables = build_tables(outer)
    anywhere = pl.BlockSpec(memory_space=pl.ANY)
    inside = pl.BlockSpec(memory_space=pltpu.VMEM)
    block = rows // seq
    wide = -(-groups * per * 8 // LANES) * LANES
    incoming = pltpu.VMEM((groups, 2, seq, block, LANES), BF16)
    returned = pltpu.VMEM((groups, seq, block, LANES), BF16)
    edge = pltpu.VMEM((seq, 1, wide), F32)
    return pl.pallas_call(
        functools.partial(operator, GRIDS[seq], seq, chan),
        out_shape=pltpu.VMEM((tokens, features), BF16),
        in_specs=[anywhere] * 12,
        out_specs=inside,
        scratch_shapes=[
            pltpu.VMEM((3, tokens, width), BF16),
            pltpu.VMEM((3, 16, width), BF16),
            pltpu.VMEM((tokens, width), F32),
            pltpu.VMEM(short_taps.shape, F32),
            pltpu.VMEM((1, width), F32),
            pltpu.VMEM(out_weight.shape, BF16),
            *(pltpu.VMEM(table.shape, table.dtype) for table in tables),
            pltpu.VMEM((3, tokens + 16, width), F32),
            pltpu.VMEM((tokens, width), F32),
            pltpu.VMEM((tokens, width), F32),
            pltpu.VMEM((rows + block, LANES), F32),
            pltpu.VMEM((wide, LANES), F32),
            edge, edge, incoming, incoming, returned, returned,
            pltpu.VMEM((2 * rows, 2 * LANES), F32),
            pltpu.VMEM((rows, 2 * LANES), BF16),
            pltpu.VMEM((rows, 2 * LANES), BF16),
            pltpu.VMEM((chan, groups, tokens, LANES), BF16),
            pltpu.VMEM((tokens, features), F32),
            pltpu.SemaphoreType.DMA((12,)),
            pltpu.SemaphoreType.DMA((2,)),
            pltpu.SemaphoreType.DMA((3 * groups + 1,)),
            pltpu.SemaphoreType.DMA((3 * groups + 1,)),
            pltpu.SemaphoreType.DMA((2, max(1, chan // 2), groups)),
            pltpu.SemaphoreType.DMA((2, max(1, chan // 2), groups)),
        ],
        compiler_params=pltpu.CompilerParams(
            collective_id=0, has_side_effects=True, vmem_limit_bytes=56 * 1024 * 1024
        ),
        cost_estimate=pl.CostEstimate(flops=2_000_000_000, bytes_accessed=5_000_000, transcendentals=0),
    )(
        query_proj, key_proj, value_proj, short_taps, kernel, skip.reshape(1, width), out_weight,
        *(jnp.asarray(table) for table in tables),
    )


def solution(mesh):
    return jax.shard_map(
        shards,
        mesh=mesh,
        in_specs=(
            P("seq", "chan"),
            P("seq", "chan"),
            P("seq", "chan"),
            P(None, None, "chan"),
            P("seq", "chan"),
            P("chan"),
            P(None, "chan"),
        ),
        out_specs=P("seq", "chan"),
        check_vma=False,
    )
```
